256 devices in a mesh: replica: 32 (over y_lo, z, core), tensor: 8 (over y_hi, x).
Axes of the slice: x: 4, y: 4 (y_hi: 2, y_lo: 2; y = y_hi * 2 + y_lo), z: 8, core: 2. Of those that a mesh axis runs over, the one named last changes fastest.
Arguments:
- queries: bfloat16 [128, 2, 8192], P('replica', None, 'tensor'), parts along dimension 0, may hold values from -16 to 16
- kv_cache: bfloat16 [2, 64, 8, 4096, 128], P(None, 'replica', 'tensor'), parts along dimension 1, may hold values from -16 to 16
- fresh_kv: bfloat16 [2, 4, 64, 8, 128], P(None, None, 'replica', 'tensor'), parts along dimension 2, may hold values from -6 to 6
- lengths: int32 [64], P('replica'), parts along dimension 0, may hold values from 512 to 4096
- spare_slot: int32 [32], P('replica'), parts along dimension 0, may hold values from 0 to 32767
- out_weight: bfloat16 [8192, 4096], P('tensor'), may hold values from -1.5 to 1.5
- residual: bfloat16 [128, 2, 4096], P('replica'), parts along dimension 0, may hold values from -3 to 3
- norm_gain: bfloat16 [4096], replicated, may hold values from 0.5 to 1.5
Outputs:
- mixed: bfloat16 [128, 2, 4096], P('replica'), parts along dimension 0
- normed: bfloat16 [128, 2, 4096], P('replica'), parts along dimension 0
The draws below stay inside these ranges and needn't reach their ends.
There are 32 independent parts, one for each index of `replica`. The reference program is written for one: setup_inputs(seed, part) draws one part's arguments, and reference() takes and returns one part's arrays. A program takes and returns all parts, laid end to end along the dimension named above; an argument that names none is the same for every part. Nothing has to cross between parts.
All inputs are finite; a program needn't handle non-finite values.
Results may differ from the reference program's by a relative error of at most 0.0058.
Values may be sent and summed in bfloat16 or wider, within the bound.
A program may use at most 64 MiB of HBM per device.

```python
import math
import jax
import jax.numpy as jnp
from jax import lax

D = 4096
HD = 128
HQ = 64
KVH = 8
STEPS = 4
ROWS = 2
CTX = 4096
N_TENSOR = 8


def draw_queries(key, part):
    key = jax.random.fold_in(key, 1)
    noise_key = jax.random.fold_in(key, 0)
    shape = (STEPS, ROWS, HQ, HD)
    values = jax.random.normal(noise_key, shape, jnp.float32)
    return values.reshape(STEPS, ROWS, HQ * HD).astype(jnp.bfloat16)


def draw_kv_cache(key, part):
    key = jax.random.fold_in(key, 2)
    shape = (2, ROWS, KVH, CTX, HD)
    values = jax.random.normal(key, shape, jnp.float32)
    return values.astype(jnp.bfloat16)


def draw_lengths(key, part):
    key = jax.random.fold_in(key, 3)
    first_key, second_key = jax.random.split(key)
    drawn = jax.random.randint(first_key, (ROWS,), CTX // 8, CTX + 1)
    longest = jax.random.randint(second_key, (), 0, ROWS)
    return jnp.where(jnp.arange(ROWS) == longest, CTX, drawn).astype(jnp.int32)


def levels(key, dims, cuts, low, top_value):
    gain = 1.0
    for dim, blocks in cuts:
        steps = jax.random.uniform(jax.random.fold_in(jax.random.fold_in(key, 6), dim), (blocks,), jnp.float32, low / len(cuts), top_value / len(cuts))
        gain = gain * jnp.repeat(jnp.exp(steps), dims[dim] // blocks).reshape((-1,) + (1,) * (len(dims) - 1 - dim))
    return gain


def centred(own_key, shape, deviation, reach, cuts=(), kind=jnp.bfloat16):
    array = jax.random.normal(own_key, shape, jnp.float32) * deviation
    if len(cuts) > 0:
        array = levels(own_key, shape, cuts, -0.22, 0.18) * array
    return jnp.clip(array, min=-reach, max=reach).astype(kind)


def setup_inputs(seed: int = 0, part: int = 0) -> dict:
    seeds = jax.random.split(jax.random.key(seed), 9)
    own_keys = jax.random.split(jax.random.fold_in(seeds[8], part), 9)
    queries = draw_queries(jax.random.fold_in(jax.random.fold_in(seeds[8], part), 71), part)
    kv_cache = draw_kv_cache(jax.random.fold_in(jax.random.fold_in(seeds[8], part), 71), part)
    fresh_kv = centred(own_keys[2], (2, STEPS, ROWS, KVH, HD), 1.0, 6.0, ((3, 8),))
    lengths = draw_lengths(jax.random.fold_in(jax.random.fold_in(seeds[8], part), 71), part)
    spare_slot = jax.random.randint(own_keys[4], (1,), 0, N_TENSOR * 4096).astype(jnp.int32)
    out_weight = centred(seeds[5], (HQ * HD, D), (max(HQ * HD // 512, 1)) ** -0.5, 1.5, ((0, 8),))
    residual = centred(own_keys[6], (STEPS, ROWS, D), 0.5, 3.0)
    norm_gain = jnp.clip(1.0 + 0.1 * jax.random.normal(seeds[7], (D,), jnp.float32), 0.5, 1.5).astype(jnp.bfloat16)
    return {"queries": queries, "kv_cache": kv_cache, "fresh_kv": fresh_kv, "lengths": lengths, "spare_slot": spare_slot, "out_weight": out_weight, "residual": residual, "norm_gain": norm_gain}


def attend(query_block, key_block, value_block, fresh_keys, fresh_values, lengths):
    scale_factor = 1.0 / math.sqrt(query_block.shape[-1])
    query_wide = query_block.astype(jnp.float32)
    cached = jnp.einsum('srgah,rgch->srgac', query_wide, key_block.astype(jnp.float32), precision=lax.Precision.HIGHEST) * scale_factor
    span_total = key_block.shape[2]
    valid_mask = jnp.arange(span_total)[None, :] < lengths[:, None]
    cached = jnp.where(valid_mask[None, :, None, None, :], cached, -1e+30)
    recent = jnp.einsum('srgah,trgh->srgat', query_wide, fresh_keys.astype(jnp.float32), precision=lax.Precision.HIGHEST) * scale_factor
    step_count = query_block.shape[0]
    causal = jnp.arange(step_count)[None, :] <= jnp.arange(step_count)[:, None]
    recent = jnp.where(causal[:, None, None, None, :], recent, -1e+30)
    highest = jnp.maximum(lax.optimization_barrier(jnp.max(cached, -1)), lax.optimization_barrier(jnp.max(recent, -1)))[..., None]
    cached_exp = jnp.exp(cached - highest)
    recent_exp = jnp.exp(recent - highest)
    totals = lax.optimization_barrier(jnp.sum(cached_exp, -1, keepdims=True)) + lax.optimization_barrier(jnp.sum(recent_exp, -1, keepdims=True))
    cached_weights = (cached_exp / totals).astype(jnp.bfloat16).astype(jnp.float32)
    recent_weights = (recent_exp / totals).astype(jnp.bfloat16).astype(jnp.float32)
    result = jnp.einsum('srgac,rgch->srgah', cached_weights, value_block.astype(jnp.float32), precision=lax.Precision.HIGHEST)
    result = result + jnp.einsum('srgat,trgh->srgah', recent_weights, fresh_values.astype(jnp.float32), precision=lax.Precision.HIGHEST)
    return result.astype(jnp.bfloat16)

def finish(stream_rows, summed, norm_gain):
    stream = stream_rows.astype(jnp.float32) + summed
    spread = lax.optimization_barrier(jnp.mean(stream * stream, -1, keepdims=True))
    normed = stream * lax.rsqrt(spread + 1e-05) * norm_gain.astype(jnp.float32)
    return (stream.astype(jnp.bfloat16), normed.astype(jnp.bfloat16))

def reference(queries, kv_cache, fresh_kv, lengths, spare_slot, out_weight, residual, norm_gain):
    offset = (spare_slot[0] % N_TENSOR * (KVH // N_TENSOR)).astype(jnp.int32)
    grouped = queries.reshape(STEPS, ROWS, KVH, HQ // KVH, HD)
    aligned = jnp.roll(grouped, offset, axis=2)
    attended = attend(aligned, kv_cache[0], kv_cache[1], fresh_kv[0], fresh_kv[1], lengths)
    restored = jnp.roll(attended, -offset, axis=2).reshape(STEPS * ROWS, HQ * HD)
    summed = jnp.dot(restored, out_weight, preferred_element_type=jnp.float32)
    mixed, normed = finish(residual.reshape(STEPS * ROWS, D), summed, norm_gain)
    return (mixed.reshape(STEPS, ROWS, D), normed.reshape(STEPS, ROWS, D))
```

```python
import functools
import math

import jax
import jax.numpy as jnp
from jax import lax
from jax.experimental import pallas as pl
from jax.experimental.pallas import tpu as pltpu
from jax.sharding import PartitionSpec as P

N = 8
PAD = 128
ORDER = (6, 5, 7, 4, 2, 1, 3)


def partner(me, offset):
    high = lax.rem(me // 4 + offset // 4, 2)
    low = lax.rem(lax.rem(me, 4) + offset % 4, 4)
    return high * 4 + low


def kernel(
    q_hbm, kv_hbm, fresh_hbm, len_hbm, spare_hbm, w_hbm, res_hbm, gain_hbm,
    mixed_out, normed_out,
    q_raw, kv, fresh_raw, len_s, spare_s, w, res_raw, gain,
    rows_f32, heads_f32, fresh_f32, q_all, o_all, sums_out, sums_in, mixed_all,
    local_sem, w_sem, send_sem, recv_sem,
):
    me = lax.axis_index("tensor")
    steps, seqs, width = q_raw.shape
    heads = width // 128
    ctx = kv_hbm.shape[2]
    cols = w.shape[1] // N

    barrier = pltpu.get_barrier_semaphore()
    for o in ORDER:
        pl.semaphore_signal(
            barrier, inc=1, device_id={"tensor": partner(me, o)},
            device_id_type=pl.DeviceIdType.MESH,
        )

    loads = [
        pltpu.make_async_copy(q_hbm, q_raw, local_sem.at[0]),
        pltpu.make_async_copy(len_hbm, len_s, local_sem.at[1]),
        pltpu.make_async_copy(spare_hbm, spare_s, local_sem.at[2]),
        pltpu.make_async_copy(fresh_hbm, fresh_raw, local_sem.at[3]),
    ]
    for part in range(2):
        for r in range(seqs):
            loads.append(
                pltpu.make_async_copy(
                    kv_hbm.at[part, r],
                    kv.at[part, r, pl.ds(0, ctx)],
                    local_sem.at[4 + 2 * part + r],
                )
            )
    loads.append(
        pltpu.make_async_copy(
            res_hbm.at[:, :, pl.ds(pl.multiple_of(me * cols, cols), cols)],
            res_raw, local_sem.at[8],
        )
    )
    loads.append(pltpu.make_async_copy(gain_hbm, gain, local_sem.at[9]))
    for copy in loads:
        copy.start()
    w_loads = []
    for piece in range(4):
        at = pl.ds(piece * w.shape[0] // 4, w.shape[0] // 4)
        copy = pltpu.make_async_copy(w_hbm.at[at], w.at[at], w_sem.at[piece])
        copy.start()
        w_loads.append(copy)

    def send(phase, src, buffer, o):
        copy = pltpu.make_async_remote_copy(
            src_ref=src, dst_ref=buffer.at[me],
            send_sem=send_sem.at[phase, o], recv_sem=recv_sem.at[phase, me],
            device_id={"tensor": partner(me, o)},
            device_id_type=pl.DeviceIdType.MESH,
        )
        copy.start()
        return copy

    def wait_arrivals(phase, buffer):
        for o in ORDER:
            source = partner(me, o)
            pltpu.make_async_remote_copy(
                src_ref=buffer.at[source], dst_ref=buffer.at[source],
                send_sem=send_sem.at[phase, o], recv_sem=recv_sem.at[phase, source],
                device_id={"tensor": source},
                device_id_type=pl.DeviceIdType.MESH,
            ).wait_recv()

    sent = []

    loads[0].wait()
    n_rows = heads * steps
    for s in range(steps):
        both = q_raw[s].astype(jnp.float32)
        for h in range(heads):
            at = (h * steps + s) * seqs
            heads_f32[at : at + seqs, :] = both[:, h * 128 : (h + 1) * 128]
    q_all[me] = jnp.concatenate(
        [heads_f32[pl.ds(r, n_rows, stride=seqs), :] for r in range(seqs)], 0
    ).astype(jnp.bfloat16)
    pl.semaphore_wait(barrier, N - 1)
    for o in ORDER:
        sent.append(send(0, q_all.at[me], q_all, o))

    loads[3].wait()
    for part in range(2):
        for t in range(steps):
            fresh_f32[part, 2 * t : 2 * t + 2, :] = fresh_raw[part, t].astype(jnp.float32)
    for part in range(2):
        for r in range(seqs):
            new = fresh_f32[part, pl.ds(r, steps, stride=seqs), :]
            tail = jnp.concatenate([new, jnp.zeros((PAD - steps, 128), jnp.float32)], 0)
            kv[part, r, ctx : ctx + PAD, :] = tail.astype(jnp.bfloat16)

    loads[1].wait()
    loads[2].wait()
    offset = jnp.bitwise_and(spare_s[0], N - 1)
    wait_arrivals(0, q_all)
    q = q_all[lax.rem(me - offset + N, N)]

    scale = math.log2(math.e) / math.sqrt(128)
    column = lax.broadcasted_iota(jnp.int32, (n_rows, ctx), 1)
    tail_column = lax.broadcasted_iota(jnp.int32, (n_rows, PAD), 1)
    tail_step = lax.rem(lax.broadcasted_iota(jnp.int32, (n_rows, PAD), 0), steps)
    for r in range(seqs):
        q_r = q[r * n_rows : (r + 1) * n_rows, :]
        loads[4 + r].wait()
        dims = (((1,), (1,)), ((), ()))
        cached = lax.dot_general(
            q_r, kv[0, r, 0:ctx, :], dims, preferred_element_type=jnp.float32
        )
        cached = jnp.where(column < len_s[r], cached, -1e30)
        recent = lax.dot_general(
            q_r, kv[0, r, ctx : ctx + PAD, :], dims, preferred_element_type=jnp.float32
        )
        recent = jnp.where(tail_column <= tail_step, recent, -1e30)
        top = jnp.maximum(
            jnp.max(cached, -1, keepdims=True), jnp.max(recent, -1, keepdims=True)
        )
        cached = jnp.exp2((cached - top) * scale)
        recent = jnp.exp2((recent - top) * scale)
        total = jnp.sum(cached, -1, keepdims=True) + jnp.sum(recent, -1, keepdims=True)
        share = 1.0 / total
        loads[6 + r].wait()
        out = jnp.dot(
            (cached * share).astype(jnp.bfloat16), kv[1, r, 0:ctx, :],
            preferred_element_type=jnp.float32,
        ) + jnp.dot(
            (recent * share).astype(jnp.bfloat16), kv[1, r, ctx : ctx + PAD, :],
            preferred_element_type=jnp.float32,
        )
        heads_f32[pl.ds(r, n_rows, stride=seqs), :] = out
    o_all[me] = heads_f32[...].astype(jnp.bfloat16)
    for o in ORDER:
        sent.append(send(1, o_all.at[me], o_all, o))
    for copy in w_loads:
        copy.wait()
    wait_arrivals(1, o_all)

    mine = o_all[lax.rem(me + offset, N)].astype(jnp.float32)
    n_out = steps * seqs
    lhs = jnp.concatenate(
        [mine[h * n_out : (h + 1) * n_out, :] for h in range(heads)], 1
    ).astype(jnp.bfloat16)

    def project(t):
        at = pl.ds(pl.multiple_of(t * cols, cols), cols)
        block = jnp.dot(lhs, w[:, at], preferred_element_type=jnp.float32)
        return jnp.concatenate([block[:, : cols // 2], block[:, cols // 2 :]], 0)

    for o in ORDER:
        sums_out[o] = project(partner(me, o)).astype(jnp.bfloat16)
        sent.append(send(2, sums_out.at[o], sums_in, o))
    stream = project(me)
    loads[8].wait()
    for s in range(steps):
        rows_f32[2 * s : 2 * s + 2, 0:cols] = res_raw[s].astype(jnp.float32)
    stream = stream + jnp.concatenate(
        [rows_f32[:, 0 : cols // 2], rows_f32[:, cols // 2 : cols]], 0
    )
    wait_arrivals(2, sums_in)
    for o in ORDER:
        stream = stream + sums_in[partner(me, o)].astype(jnp.float32)

    mixed_all[me] = stream.astype(jnp.bfloat16)
    for o in ORDER:
        sent.append(send(3, mixed_all.at[me], mixed_all, o))
    loads[9].wait()
    wait_arrivals(3, mixed_all)
    blocks = []
    for t in range(N):
        block = mixed_all[t].astype(jnp.float32)
        blocks += [block[:n_out], block[n_out:]]
    whole = jnp.concatenate(blocks, 1)
    spread = jnp.sum(whole * whole, -1, keepdims=True) * (1.0 / whole.shape[1])
    normed = whole * lax.rsqrt(spread + 1e-05) * gain[...].astype(jnp.float32)[None, :]
    for s in range(steps):
        mixed_out[s] = whole[2 * s : 2 * s + 2, :].astype(jnp.bfloat16)
        normed_out[s] = normed[2 * s : 2 * s + 2, :].astype(jnp.bfloat16)
    for copy in sent:
        copy.wait_send()


def shards(queries, kv_cache, fresh_kv, lengths, spare_slot, out_weight, residual, norm_gain):
    steps, seqs, width = queries.shape
    ctx = kv_cache.shape[3]
    features = out_weight.shape[1]
    heads = width // 128
    cols = features // N
    bf16, f32 = jnp.bfloat16, jnp.float32
    out = jax.ShapeDtypeStruct((steps, seqs, features), bf16)
    block = (2 * steps * seqs, cols // 2)
    return pl.pallas_call(
        kernel,
        out_shape=(out, out),
        in_specs=[pl.BlockSpec(memory_space=pltpu.HBM)] * 8,
        out_specs=(pl.BlockSpec(memory_space=pltpu.VMEM),) * 2,
        scratch_shapes=[
            pltpu.VMEM((steps, seqs, width), bf16),
            pltpu.VMEM((2, seqs, ctx + PAD, 128), bf16),
            pltpu.VMEM((2, steps, seqs, 128), bf16),
            pltpu.SMEM((seqs,), jnp.int32),
            pltpu.SMEM((1,), jnp.int32),
            pltpu.VMEM((width, features), bf16),
            pltpu.VMEM((steps, seqs, cols), bf16),
            pltpu.VMEM((features,), bf16),
            pltpu.VMEM((steps * seqs, cols), f32),
            pltpu.VMEM((seqs * heads * steps, 128), f32),
            pltpu.VMEM((2, steps * seqs, 128), f32),
            pltpu.VMEM((N, seqs * heads * steps, 128), bf16),
            pltpu.VMEM((N, seqs * heads * steps, 128), bf16),
            pltpu.VMEM((N,) + block, bf16),
            pltpu.VMEM((N,) + block, bf16),
            pltpu.VMEM((N,) + block, bf16),
            pltpu.SemaphoreType.DMA((10,)),
            pltpu.SemaphoreType.DMA((4,)),
            pltpu.SemaphoreType.DMA((4, N)),
            pltpu.SemaphoreType.DMA((4, N)),
        ],
        compiler_params=pltpu.CompilerParams(
            collective_id=0, has_side_effects=True, vmem_limit_bytes=56 * 2**20
        ),
    )(
        queries,
        kv_cache.reshape(2, seqs, ctx, 128),
        fresh_kv.reshape(2, steps, seqs, 128),
        lengths,
        spare_slot,
        out_weight,
        residual,
        norm_gain,
    )


def solution(mesh):
    return jax.shard_map(
        shards,
        mesh=mesh,
        in_specs=(
            P("replica", None, "tensor"),
            P(None, "replica", "tensor", None, None),
            P(None, None, "replica", "tensor", None),
            P("replica"),
            P("replica"),
            P("tensor", None),
            P("replica", None, None),
            P(),
        ),
        out_specs=(P("replica", None, None), P("replica", None, None)),
        check_vma=False,
    )
```

```python
import functools
import math

import jax
import jax.numpy as jnp
from jax import lax
from jax.experimental import pallas as pl
from jax.experimental.pallas import tpu as pltpu
from jax.sharding import PartitionSpec as P

N = 8
PAD = 128
WIDE = 4
ORDER = (6, 5, 7, 4, 2, 1, 3)
ALONG_X = (2, 1, 3)


def partner(me, offset):
    high = lax.rem(me // 4 + offset // 4, 2)
    low = lax.rem(lax.rem(me, 4) + offset % 4, 4)
    return high * 4 + low


def kernel(
    q_hbm, kv_hbm, fresh_hbm, len_hbm, spare_hbm, w_hbm, res_hbm, gain_hbm,
    blocks_out, res_out, gain_out,
    q_raw, kv, fresh_raw, len_s, spare_s, w, res_raw, gain_raw,
    heads_f32, fresh_f32, q_all, o_all, sums_out, sums_in,
    local_sem, w_sem, send_sem, recv_sem,
):
    me = lax.axis_index("tensor")
    steps, seqs, width = q_raw.shape
    heads = width // 128
    ctx = kv_hbm.shape[2]
    cols = w.shape[1] // WIDE

    barrier = pltpu.get_barrier_semaphore()
    for o in ORDER:
        pl.semaphore_signal(
            barrier, inc=1, device_id={"tensor": partner(me, o)},
            device_id_type=pl.DeviceIdType.MESH,
        )

    loads = [
        pltpu.make_async_copy(q_hbm, q_raw, local_sem.at[0]),
        pltpu.make_async_copy(len_hbm, len_s, local_sem.at[1]),
        pltpu.make_async_copy(spare_hbm, spare_s, local_sem.at[2]),
        pltpu.make_async_copy(fresh_hbm, fresh_raw, local_sem.at[3]),
    ]
    for part in range(2):
        for r in range(seqs):
            loads.append(
                pltpu.make_async_copy(
                    kv_hbm.at[part, r],
                    kv.at[part, r, pl.ds(0, ctx)],
                    local_sem.at[4 + 2 * part + r],
                )
            )
    loads.append(pltpu.make_async_copy(res_hbm, res_raw, local_sem.at[8]))
    loads.append(pltpu.make_async_copy(gain_hbm, gain_raw, local_sem.at[9]))
    for copy in loads:
        copy.start()
    w_loads = []
    for piece in range(4):
        at = pl.ds(piece * w.shape[0] // 4, w.shape[0] // 4)
        copy = pltpu.make_async_copy(w_hbm.at[at], w.at[at], w_sem.at[piece])
        copy.start()
        w_loads.append(copy)

    def send(phase, src, dst, slot, o):
        copy = pltpu.make_async_remote_copy(
            src_ref=src, dst_ref=dst.at[slot],
            send_sem=send_sem.at[phase, o], recv_sem=recv_sem.at[phase, slot],
            device_id={"tensor": partner(me, o)},
            device_id_type=pl.DeviceIdType.MESH,
        )
        copy.start()
        return copy

    def wait_arrival(phase, dst, slot, o):
        pltpu.make_async_remote_copy(
            src_ref=dst.at[slot], dst_ref=dst.at[slot],
            send_sem=send_sem.at[phase, o], recv_sem=recv_sem.at[phase, slot],
            device_id={"tensor": partner(me, o)},
            device_id_type=pl.DeviceIdType.MESH,
        ).wait_recv()

    sent = []

    loads[0].wait()
    n_rows = heads * steps
    for s in range(steps):
        both = q_raw[s].astype(jnp.float32)
        for h in range(heads):
            at = (h * steps + s) * seqs
            heads_f32[at : at + seqs, :] = both[:, h * 128 : (h + 1) * 128]
    q_all[me] = jnp.concatenate(
        [heads_f32[pl.ds(r, n_rows, stride=seqs), :] for r in range(seqs)], 0
    ).astype(jnp.bfloat16)
    pl.semaphore_wait(barrier, N - 1)
    for o in ORDER:
        sent.append(send(0, q_all.at[me], q_all, me, o))

    loads[3].wait()
    for part in range(2):
        for t in range(steps):
            fresh_f32[part, 2 * t : 2 * t + 2, :] = fresh_raw[part, t].astype(jnp.float32)
    for part in range(2):
        for r in range(seqs):
            new = fresh_f32[part, pl.ds(r, steps, stride=seqs), :]
            tail = jnp.concatenate([new, jnp.zeros((PAD - steps, 128), jnp.float32)], 0)
            kv[part, r, ctx : ctx + PAD, :] = tail.astype(jnp.bfloat16)

    loads[8].wait()
    for s in range(steps):
        res_out[2 * s : 2 * s + 2, :] = res_raw[s].astype(jnp.float32)
    loads[9].wait()
    gain_out[...] = jnp.broadcast_to(
        gain_raw[...].astype(jnp.float32)[None, :], gain_out.shape
    )

    loads[1].wait()
    loads[2].wait()
    offset = jnp.bitwise_and(spare_s[0], N - 1)
    for o in ORDER:
        wait_arrival(0, q_all, partner(me, o), o)
    q = q_all[lax.rem(me - offset + N, N)]

    scale = math.log2(math.e) / math.sqrt(128)
    column = lax.broadcasted_iota(jnp.int32, (n_rows, ctx), 1)
    tail_column = lax.broadcasted_iota(jnp.int32, (n_rows, PAD), 1)
    tail_step = lax.rem(lax.broadcasted_iota(jnp.int32, (n_rows, PAD), 0), steps)
    for r in range(seqs):
        q_r = q[r * n_rows : (r + 1) * n_rows, :]
        loads[4 + r].wait()
        dims = (((1,), (1,)), ((), ()))
        cached = lax.dot_general(
            q_r, kv[0, r, 0:ctx, :], dims, preferred_element_type=jnp.float32
        )
        cached = jnp.where(column < len_s[r], cached, -1e30)
        recent = lax.dot_general(
            q_r, kv[0, r, ctx : ctx + PAD, :], dims, preferred_element_type=jnp.float32
        )
        recent = jnp.where(tail_column <= tail_step, recent, -1e30)
        top = jnp.maximum(
            jnp.max(cached, -1, keepdims=True), jnp.max(recent, -1, keepdims=True)
        )
        cached = jnp.exp2((cached - top) * scale)
        recent = jnp.exp2((recent - top) * scale)
        total = jnp.sum(cached, -1, keepdims=True) + jnp.sum(recent, -1, keepdims=True)
        share = 1.0 / total
        loads[6 + r].wait()
        out = jnp.dot(
            (cached * share).astype(jnp.bfloat16), kv[1, r, 0:ctx, :],
            preferred_element_type=jnp.float32,
        ) + jnp.dot(
            (recent * share).astype(jnp.bfloat16), kv[1, r, ctx : ctx + PAD, :],
            preferred_element_type=jnp.float32,
        )
        heads_f32[pl.ds(r, n_rows, stride=seqs), :] = out
    o_all[me] = heads_f32[...].astype(jnp.bfloat16)
    for o in ORDER:
        sent.append(send(1, o_all.at[me], o_all, me, o))
    for copy in w_loads:
        copy.wait()
    for o in ORDER:
        wait_arrival(1, o_all, partner(me, o), o)

    mine = o_all[lax.rem(me + offset, N)].astype(jnp.float32)
    n_out = steps * seqs
    lhs = jnp.concatenate(
        [mine[h * n_out : (h + 1) * n_out, :] for h in range(heads)], 1
    ).astype(jnp.bfloat16)

    def project(x):
        at = pl.ds(pl.multiple_of(x * cols, cols), cols)
        block = jnp.dot(lhs, w[:, at], preferred_element_type=jnp.float32)
        return jnp.concatenate([block[:, : cols // 2], block[:, cols // 2 :]], 0)

    x_me = lax.rem(me, WIDE)
    for o in ALONG_X:
        sums_out[o] = project(lax.rem(x_me + o, WIDE)).astype(jnp.bfloat16)
        sent.append(send(2, sums_out.at[o], sums_in, x_me, o))
    block = project(x_me)
    for o in ALONG_X:
        x = lax.rem(x_me + o, WIDE)
        wait_arrival(2, sums_in, x, o)
        block = block + sums_in[x].astype(jnp.float32)

    blocks_out[me] = block.astype(jnp.bfloat16)
    for o in ORDER:
        sent.append(send(3, blocks_out.at[me], blocks_out, me, o))
    for o in ORDER:
        wait_arrival(3, blocks_out, partner(me, o), o)
    for copy in sent:
        copy.wait_send()


def finish(blocks, res, gain, mixed_hbm, normed_hbm, mixed, normed, sems):
    steps, seqs, width = mixed_hbm.shape
    rows = steps * seqs
    parts = []
    for x in range(WIDE):
        both = blocks[x].astype(jnp.float32) + blocks[WIDE + x].astype(jnp.float32)
        parts += [both[:rows], both[rows:]]
    stream = jnp.concatenate(parts, 1) + res[...]
    for s in range(steps):
        mixed[s] = stream[seqs * s : seqs * (s + 1), :].astype(jnp.bfloat16)
    first = pltpu.make_async_copy(mixed, mixed_hbm, sems.at[0])
    first.start()
    spread = jnp.sum(stream * stream, -1, keepdims=True) * (1.0 / width)
    scaled = stream * lax.rsqrt(spread + 1e-05) * gain[...]
    for s in range(steps):
        normed[s] = scaled[seqs * s : seqs * (s + 1), :].astype(jnp.bfloat16)
    second = pltpu.make_async_copy(normed, normed_hbm, sems.at[1])
    second.start()
    first.wait()
    second.wait()


def pinned(array):
    if array.size == 1:
        return array
    return pltpu.with_memory_space_constraint(array, pltpu.HBM)


def shards(queries, kv_cache, fresh_kv, lengths, spare_slot, out_weight, residual, norm_gain):
    steps, seqs, width = queries.shape
    ctx = kv_cache.shape[3]
    features = out_weight.shape[1]
    heads = width // 128
    cols = features // WIDE
    bf16, f32 = jnp.bfloat16, jnp.float32
    rows = steps * seqs
    block = (2 * rows, cols // 2)
    args = [
        queries,
        kv_cache.reshape(2, seqs, ctx, 128),
        fresh_kv.reshape(2, steps, seqs, 128),
        lengths,
        spare_slot,
        out_weight,
        residual,
        norm_gain,
    ]
    blocks, res, gain = pl.pallas_call(
        kernel,
        out_shape=(
            pltpu.VMEM((N,) + block, bf16),
            pltpu.VMEM((rows, features), f32),
            pltpu.VMEM((rows, features), f32),
        ),
        in_specs=[pl.BlockSpec(memory_space=pltpu.HBM)] * 8,
        out_specs=(pl.BlockSpec(memory_space=pltpu.VMEM),) * 3,
        scratch_shapes=[
            pltpu.VMEM((steps, seqs, width), bf16),
            pltpu.VMEM((2, seqs, ctx + PAD, 128), bf16),
            pltpu.VMEM((2, steps, seqs, 128), bf16),
            pltpu.SMEM((seqs,), jnp.int32),
            pltpu.SMEM((1,), jnp.int32),
            pltpu.VMEM((width, features), bf16),
            pltpu.VMEM((steps, seqs, features), bf16),
            pltpu.VMEM((features,), bf16),
            pltpu.VMEM((heads * rows, 128), f32),
            pltpu.VMEM((2, rows, 128), f32),
            pltpu.VMEM((N, heads * rows, 128), bf16),
            pltpu.VMEM((N, heads * rows, 128), bf16),
            pltpu.VMEM((WIDE,) + block, bf16),
            pltpu.VMEM((WIDE,) + block, bf16),
            pltpu.SemaphoreType.DMA((10,)),
            pltpu.SemaphoreType.DMA((4,)),
            pltpu.SemaphoreType.DMA((4, N)),
            pltpu.SemaphoreType.DMA((4, N)),
        ],
        compiler_params=pltpu.CompilerParams(
            collective_id=0, has_side_effects=True, vmem_limit_bytes=32 * 2**20
        ),
    )(*[pinned(a) for a in args])
    out = pltpu.HBM((steps, seqs, features), bf16)
    return pl.pallas_call(
        finish,
        out_shape=(out, out),
        in_specs=[pl.BlockSpec(memory_space=pltpu.VMEM)] * 3,
        out_specs=(pl.BlockSpec(memory_space=pltpu.HBM),) * 2,
        scratch_shapes=[
            pltpu.VMEM((steps, seqs, features), bf16),
            pltpu.VMEM((steps, seqs, features), bf16),
            pltpu.SemaphoreType.DMA((2,)),
        ],
        compiler_params=pltpu.CompilerParams(vmem_limit_bytes=8 * 2**20),
    )(*[pltpu.with_memory_space_constraint(a, pltpu.VMEM) for a in (blocks, res, gain)])


def solution(mesh):
    return jax.shard_map(
        shards,
        mesh=mesh,
        in_specs=(
            P("replica", None, "tensor"),
            P(None, "replica", "tensor", None, None),
            P(None, None, "replica", "tensor", None),
            P("replica"),
            P("replica"),
            P("tensor", None),
            P("replica", None, None),
            P(),
        ),
        out_specs=(P("replica", None, None), P("replica", None, None)),
        check_vma=False,
    )
```

```python
import functools
import math

import jax
import jax.numpy as jnp
from jax import lax
from jax.experimental import pallas as pl
from jax.experimental.pallas import tpu as pltpu
from jax.sharding import PartitionSpec as P

N = 8
PAD = 128
WIDE = 4
PIECES = 4
ORDER = (6, 5, 7, 4, 2, 1, 3)


def partner(me, offset):
    high = lax.rem(me // 4 + offset // 4, 2)
    low = lax.rem(lax.rem(me, 4) + offset % 4, 4)
    return high * 4 + low


def slot_of(me, source):
    high = lax.rem(me // WIDE + source // WIDE, 2)
    low = lax.rem(lax.rem(me, WIDE) - lax.rem(source, WIDE) + WIDE, WIDE)
    return high * WIDE + low


def kernel(
    q_hbm, kv_hbm, fresh_hbm, len_hbm, spare_hbm, w_hbm, res_hbm, gain_hbm,
    sums, res_out, gain_out,
    q_raw, kv, fresh_raw, len_s, spare_s, w, res_raw, gain_raw,
    heads_f32, fresh_f32, q_all, o_all,
    local_sem, w_sem, send_sem, recv_sem,
):
    me = lax.axis_index("tensor")
    steps, seqs, width = q_raw.shape
    heads = width // 128
    ctx = kv_hbm.shape[2]

    barrier = pltpu.get_barrier_semaphore()
    for o in ORDER:
        pl.semaphore_signal(
            barrier, inc=1, device_id={"tensor": partner(me, o)},
            device_id_type=pl.DeviceIdType.MESH,
        )

    loads = [
        pltpu.make_async_copy(q_hbm, q_raw, local_sem.at[0]),
        pltpu.make_async_copy(len_hbm, len_s, local_sem.at[1]),
        pltpu.make_async_copy(spare_hbm, spare_s, local_sem.at[2]),
        pltpu.make_async_copy(fresh_hbm, fresh_raw, local_sem.at[3]),
    ]
    for part in range(2):
        for r in range(seqs):
            loads.append(
                pltpu.make_async_copy(
                    kv_hbm.at[part, r],
                    kv.at[part, r, pl.ds(0, ctx)],
                    local_sem.at[4 + 2 * part + r],
                )
            )
    loads.append(pltpu.make_async_copy(res_hbm, res_raw, local_sem.at[8]))
    loads.append(pltpu.make_async_copy(gain_hbm, gain_raw, local_sem.at[9]))
    for copy in loads:
        copy.start()
    w_loads = []
    for piece in range(4):
        at = pl.ds(piece * w.shape[0] // 4, w.shape[0] // 4)
        copy = pltpu.make_async_copy(w_hbm.at[at], w.at[at], w_sem.at[piece])
        copy.start()
        w_loads.append(copy)

    def send(phase, slots, o, piece=None):
        src, dst = slots.at[0], slots.at[o]
        if piece is not None:
            src, dst = src.at[piece], dst.at[piece]
        copy = pltpu.make_async_remote_copy(
            src_ref=src, dst_ref=dst,
            send_sem=send_sem.at[phase], recv_sem=recv_sem.at[phase],
            device_id={"tensor": partner(me, o)},
            device_id_type=pl.DeviceIdType.MESH,
        )
        copy.start()

    def whole(phase, slots):
        others = slots.at[pl.ds(1, N - 1)]
        return pltpu.make_async_remote_copy(
            src_ref=others, dst_ref=others,
            send_sem=send_sem.at[phase], recv_sem=recv_sem.at[phase],
            device_id={"tensor": partner(me, 1)},
            device_id_type=pl.DeviceIdType.MESH,
        )

    loads[0].wait()
    n_rows = heads * steps
    for s in range(steps):
        both = q_raw[s].astype(jnp.float32)
        for h in range(heads):
            at = (h * steps + s) * seqs
            heads_f32[at : at + seqs, :] = both[:, h * 128 : (h + 1) * 128]
    q_all[0] = jnp.concatenate(
        [heads_f32[pl.ds(r, n_rows, stride=seqs), :] for r in range(seqs)], 0
    ).astype(jnp.bfloat16)
    pl.semaphore_wait(barrier, N - 1)
    for o in ORDER:
        send(0, q_all, o)

    loads[3].wait()
    for part in range(2):
        for t in range(steps):
            fresh_f32[part, 2 * t : 2 * t + 2, :] = fresh_raw[part, t].astype(jnp.float32)
    for part in range(2):
        for r in range(seqs):
            new = fresh_f32[part, pl.ds(r, steps, stride=seqs), :]
            tail = jnp.concatenate([new, jnp.zeros((PAD - steps, 128), jnp.float32)], 0)
            kv[part, r, ctx : ctx + PAD, :] = tail.astype(jnp.bfloat16)

    loads[8].wait()
    for s in range(steps):
        res_out[2 * s : 2 * s + 2, :] = res_raw[s].astype(jnp.float32)
    loads[9].wait()
    gain_out[...] = jnp.broadcast_to(
        gain_raw[...].astype(jnp.float32)[None, :], gain_out.shape
    )

    loads[1].wait()
    loads[2].wait()
    offset = jnp.bitwise_and(spare_s[0], N - 1)
    whole(0, q_all).wait_recv()
    q = q_all[slot_of(me, lax.rem(me - offset + N, N))]

    scale = math.log2(math.e) / math.sqrt(128)
    column = lax.broadcasted_iota(jnp.int32, (n_rows, ctx), 1)
    tail_column = lax.broadcasted_iota(jnp.int32, (n_rows, PAD), 1)
    tail_step = lax.rem(lax.broadcasted_iota(jnp.int32, (n_rows, PAD), 0), steps)
    for r in range(seqs):
        q_r = q[r * n_rows : (r + 1) * n_rows, :]
        loads[4 + r].wait()
        dims = (((1,), (1,)), ((), ()))
        cached = lax.dot_general(
            q_r, kv[0, r, 0:ctx, :], dims, preferred_element_type=jnp.float32
        )
        cached = jnp.where(column < len_s[r], cached, -1e30)
        recent = lax.dot_general(
            q_r, kv[0, r, ctx : ctx + PAD, :], dims, preferred_element_type=jnp.float32
        )
        recent = jnp.where(tail_column <= tail_step, recent, -1e30)
        top = jnp.maximum(
            jnp.max(cached, -1, keepdims=True), jnp.max(recent, -1, keepdims=True)
        )
        cached = jnp.exp2((cached - top) * scale)
        recent = jnp.exp2((recent - top) * scale)
        total = jnp.sum(cached, -1, keepdims=True) + jnp.sum(recent, -1, keepdims=True)
        share = 1.0 / total
        loads[6 + r].wait()
        out = jnp.dot(
            (cached * share).astype(jnp.bfloat16), kv[1, r, 0:ctx, :],
            preferred_element_type=jnp.float32,
        ) + jnp.dot(
            (recent * share).astype(jnp.bfloat16), kv[1, r, ctx : ctx + PAD, :],
            preferred_element_type=jnp.float32,
        )
        heads_f32[pl.ds(r, n_rows, stride=seqs), :] = out
    o_all[0] = heads_f32[...].astype(jnp.bfloat16)
    for o in ORDER:
        send(1, o_all, o)
    for copy in w_loads:
        copy.wait()
    whole(1, o_all).wait_recv()

    mine = o_all[slot_of(me, lax.rem(me + offset, N))].astype(jnp.float32)
    n_out = steps * seqs
    lhs = jnp.concatenate(
        [mine[h * n_out : (h + 1) * n_out, :] for h in range(heads)], 1
    ).astype(jnp.bfloat16)

    cols = w.shape[1] // PIECES
    for piece in range(PIECES):
        at = pl.ds(piece * cols, cols)
        block = jnp.dot(lhs, w[:, at], preferred_element_type=jnp.float32)
        sums[0, piece] = jnp.concatenate(
            [block[:, : cols // 2], block[:, cols // 2 :]], 0
        ).astype(jnp.bfloat16)
        for o in ORDER:
            send(2, sums, o, piece)
    whole(2, sums).wait_recv()
    for phase, slots in enumerate((q_all, o_all, sums)):
        whole(phase, slots).wait_send()


def finish(sums, res, gain, mixed_hbm, normed_hbm, mixed, normed, sems):
    steps, seqs, width = mixed_hbm.shape
    rows = steps * seqs
    parts = []
    for piece in range(PIECES):
        total = sums[0, piece].astype(jnp.float32)
        for slot in range(1, N):
            total = total + sums[slot, piece].astype(jnp.float32)
        parts += [total[:rows], total[rows:]]
    stream = jnp.concatenate(parts, 1) + res[...]
    for s in range(steps):
        mixed[s] = stream[seqs * s : seqs * (s + 1), :].astype(jnp.bfloat16)
    first = pltpu.make_async_copy(mixed, mixed_hbm, sems.at[0])
    first.start()
    spread = jnp.sum(stream * stream, -1, keepdims=True) * (1.0 / width)
    scaled = stream * lax.rsqrt(spread + 1e-05) * gain[...]
    for s in range(steps):
        normed[s] = scaled[seqs * s : seqs * (s + 1), :].astype(jnp.bfloat16)
    second = pltpu.make_async_copy(normed, normed_hbm, sems.at[1])
    second.start()
    first.wait()
    second.wait()


def pinned(array):
    if array.size == 1:
        return array
    return pltpu.with_memory_space_constraint(array, pltpu.HBM)


def shards(queries, kv_cache, fresh_kv, lengths, spare_slot, out_weight, residual, norm_gain):
    steps, seqs, width = queries.shape
    ctx = kv_cache.shape[3]
    features = out_weight.shape[1]
    heads = width // 128
    cols = features // PIECES
    bf16, f32 = jnp.bfloat16, jnp.float32
    rows = steps * seqs
    block = (2 * rows, cols // 2)
    args = [
        queries,
        kv_cache.reshape(2, seqs, ctx, 128),
        fresh_kv.reshape(2, steps, seqs, 128),
        lengths,
        spare_slot,
        out_weight,
        residual,
        norm_gain,
    ]
    sums, res, gain = pl.pallas_call(
        kernel,
        out_shape=(
            pltpu.VMEM((N, PIECES) + block, bf16),
            pltpu.VMEM((rows, features), f32),
            pltpu.VMEM((rows, features), f32),
        ),
        in_specs=[pl.BlockSpec(memory_space=pltpu.HBM)] * 8,
        out_specs=(pl.BlockSpec(memory_space=pltpu.VMEM),) * 3,
        scratch_shapes=[
            pltpu.VMEM((steps, seqs, width), bf16),
            pltpu.VMEM((2, seqs, ctx + PAD, 128), bf16),
            pltpu.VMEM((2, steps, seqs, 128), bf16),
            pltpu.SMEM((seqs,), jnp.int32),
            pltpu.SMEM((1,), jnp.int32),
            pltpu.VMEM((width, features), bf16),
            pltpu.VMEM((steps, seqs, features), bf16),
            pltpu.VMEM((features,), bf16),
            pltpu.VMEM((heads * rows, 128), f32),
            pltpu.VMEM((2, rows, 128), f32),
            pltpu.VMEM((N, heads * rows, 128), bf16),
            pltpu.VMEM((N, heads * rows, 128), bf16),
            pltpu.SemaphoreType.DMA((10,)),
            pltpu.SemaphoreType.DMA((4,)),
            pltpu.SemaphoreType.DMA((3,)),
            pltpu.SemaphoreType.DMA((3,)),
        ],
        compiler_params=pltpu.CompilerParams(
            collective_id=0, has_side_effects=True, vmem_limit_bytes=32 * 2**20
        ),
    )(*[pinned(a) for a in args])
    out = pltpu.HBM((steps, seqs, features), bf16)
    return pl.pallas_call(
        finish,
        out_shape=(out, out),
        in_specs=[pl.BlockSpec(memory_space=pltpu.VMEM)] * 3,
        out_specs=(pl.BlockSpec(memory_space=pltpu.HBM),) * 2,
        scratch_shapes=[
            pltpu.VMEM((steps, seqs, features), bf16),
            pltpu.VMEM((steps, seqs, features), bf16),
            pltpu.SemaphoreType.DMA((2,)),
        ],
        compiler_params=pltpu.CompilerParams(vmem_limit_bytes=8 * 2**20),
    )(*[pltpu.with_memory_space_constraint(a, pltpu.VMEM) for a in (sums, res, gain)])


def solution(mesh):
    return jax.shard_map(
        shards,
        mesh=mesh,
        in_specs=(
            P("replica", None, "tensor"),
            P(None, "replica", "tensor", None, None),
            P(None, None, "replica", "tensor", None),
            P("replica"),
            P("replica"),
            P("tensor", None),
            P("replica", None, None),
            P(),
        ),
        out_specs=(P("replica", None, None), P("replica", None, None)),
        check_vma=False,
    )
```

```python
import functools
import math

import jax
import jax.numpy as jnp
from jax import lax
from jax.experimental import pallas as pl
from jax.experimental.pallas import tpu as pltpu
from jax.sharding import PartitionSpec as P

N = 8
PAD = 128
WIDE = 4
PIECES = 4
ORDER = (6, 5, 7, 4, 2, 1, 3)


def partner(me, offset):
    high = lax.rem(me // 4 + offset // 4, 2)
    low = lax.rem(lax.rem(me, 4) + offset % 4, 4)
    return high * 4 + low


def slot_of(me, source):
    high = lax.rem(me // WIDE + source // WIDE, 2)
    low = lax.rem(lax.rem(me, WIDE) - lax.rem(source, WIDE) + WIDE, WIDE)
    return high * WIDE + low


def kernel(
    q_hbm, kv_hbm, fresh_hbm, len_hbm, spare_hbm, w_hbm, res_hbm, gain_hbm,
    sums, res_out, gain_out,
    q_raw, keys, values, k_turned, fresh_raw, len_s, spare_s, w, res_raw, gain_raw,
    heads_f32, fresh_f32, q_all, o_all,
    local_sem, w_sem, send_sem, recv_sem,
):
    me = lax.axis_index("tensor")
    steps, seqs, width = q_raw.shape
    heads = width // 128
    ctx = kv_hbm.shape[2]

    barrier = pltpu.get_barrier_semaphore()
    for o in ORDER:
        pl.semaphore_signal(
            barrier, inc=1, device_id={"tensor": partner(me, o)},
            device_id_type=pl.DeviceIdType.MESH,
        )

    loads = [
        pltpu.make_async_copy(q_hbm, q_raw, local_sem.at[0]),
        pltpu.make_async_copy(len_hbm, len_s, local_sem.at[1]),
        pltpu.make_async_copy(spare_hbm, spare_s, local_sem.at[2]),
        pltpu.make_async_copy(fresh_hbm, fresh_raw, local_sem.at[3]),
    ]
    for part in range(2):
        for r in range(seqs):
            loads.append(
                pltpu.make_async_copy(
                    kv_hbm.at[part, r],
                    (keys, values)[part].at[pl.ds(0, ctx), pl.ds(r * 128, 128)],
                    local_sem.at[4 + 2 * part + r],
                )
            )
    loads.append(pltpu.make_async_copy(res_hbm, res_raw, local_sem.at[8]))
    loads.append(pltpu.make_async_copy(gain_hbm, gain_raw, local_sem.at[9]))
    for copy in loads:
        copy.start()
    w_loads = []
    for piece in range(4):
        at = pl.ds(piece * w.shape[0] // 4, w.shape[0] // 4)
        copy = pltpu.make_async_copy(w_hbm.at[at], w.at[at], w_sem.at[piece])
        copy.start()
        w_loads.append(copy)

    def send(phase, slots, o, piece=None):
        src, dst = slots.at[0], slots.at[o]
        if piece is not None:
            src, dst = src.at[piece], dst.at[piece]
        copy = pltpu.make_async_remote_copy(
            src_ref=src, dst_ref=dst,
            send_sem=send_sem.at[phase], recv_sem=recv_sem.at[phase],
            device_id={"tensor": partner(me, o)},
            device_id_type=pl.DeviceIdType.MESH,
        )
        copy.start()

    def whole(phase, slots):
        others = slots.at[pl.ds(1, N - 1)]
        return pltpu.make_async_remote_copy(
            src_ref=others, dst_ref=others,
            send_sem=send_sem.at[phase], recv_sem=recv_sem.at[phase],
            device_id={"tensor": partner(me, 1)},
            device_id_type=pl.DeviceIdType.MESH,
        )

    loads[0].wait()
    n_rows = heads * steps
    for s in range(steps):
        both = q_raw[s].astype(jnp.float32)
        for h in range(heads):
            at = (h * steps + s) * seqs
            heads_f32[at : at + seqs, :] = both[:, h * 128 : (h + 1) * 128]
    q_all[0] = jnp.concatenate(
        [heads_f32[pl.ds(r, n_rows, stride=seqs), :] for r in range(seqs)], 0
    ).astype(jnp.bfloat16)
    pl.semaphore_wait(barrier, N - 1)
    for o in ORDER:
        send(0, q_all, o)

    loads[3].wait()
    for part in range(2):
        for t in range(steps):
            fresh_f32[part, 2 * t : 2 * t + 2, :] = fresh_raw[part, t].astype(jnp.float32)
    for part in range(2):
        for r in range(seqs):
            new = fresh_f32[part, pl.ds(r, steps, stride=seqs), :]
            tail = jnp.concatenate([new, jnp.zeros((PAD - steps, 128), jnp.float32)], 0)
            (keys, values)[part][ctx : ctx + PAD, r * 128 : (r + 1) * 128] = tail.astype(
                jnp.bfloat16
            )

    for r in range(seqs):
        loads[4 + r].wait()
    for low in range(0, ctx + PAD, 128):
        k_turned[:, low : low + 128] = keys[low : low + 128, :].T

    loads[8].wait()
    for s in range(steps):
        res_out[2 * s : 2 * s + 2, :] = res_raw[s].astype(jnp.float32)
    loads[9].wait()
    gain_out[...] = jnp.broadcast_to(
        gain_raw[...].astype(jnp.float32)[None, :], gain_out.shape
    )

    loads[1].wait()
    loads[2].wait()
    offset = jnp.bitwise_and(spare_s[0], N - 1)
    whole(0, q_all).wait_recv()
    q = q_all[slot_of(me, lax.rem(me - offset + N, N))]

    scale = math.log2(math.e) / math.sqrt(128)
    none = jnp.zeros((n_rows, 128), q.dtype)
    diagonal = jnp.concatenate(
        [
            jnp.concatenate([q[:n_rows], none], 1),
            jnp.concatenate([none, q[n_rows:]], 1),
        ],
        0,
    )
    row = lax.broadcasted_iota(jnp.int32, (seqs * n_rows, 1), 0)
    limit = jnp.where(row < n_rows, len_s[0], len_s[1])
    step = lax.rem(row, steps)
    top = total = out = None
    half = ctx // 2 + PAD
    for low, high in ((0, half), (half, ctx + PAD)):
        scores = jnp.dot(
            diagonal, k_turned[:, low:high], preferred_element_type=jnp.float32
        )
        end = min(high, ctx) - low
        column = lax.broadcasted_iota(jnp.int32, (seqs * n_rows, end), 1)
        masked = jnp.where(column < limit - low, scores[:, :end], -1e30)
        if high > ctx:
            column = lax.broadcasted_iota(jnp.int32, (seqs * n_rows, PAD), 1)
            recent = jnp.where(column <= step, scores[:, end:], -1e30)
            masked = jnp.concatenate([masked, recent], 1)
        highest = jnp.max(masked, -1, keepdims=True)
        if low > 0:
            highest = jnp.maximum(top, highest)
        weights = jnp.exp2((masked - highest) * scale)
        part_total = jnp.sum(weights, -1, keepdims=True)
        if low == 0:
            for r in range(seqs):
                loads[6 + r].wait()
        part_out = jnp.dot(
            weights.astype(jnp.bfloat16), values[low:high, :],
            preferred_element_type=jnp.float32,
        )
        if low > 0:
            shrink = jnp.exp2((top - highest) * scale)
            part_total = part_total + total * shrink
            part_out = part_out + out * shrink
        top, total, out = highest, part_total, part_out
    share = 1.0 / total
    for r in range(seqs):
        mine = slice(r * n_rows, (r + 1) * n_rows)
        heads_f32[pl.ds(r, n_rows, stride=seqs), :] = (
            out[mine, r * 128 : (r + 1) * 128] * share[mine]
        )
    o_all[0] = heads_f32[...].astype(jnp.bfloat16)
    for o in ORDER:
        send(1, o_all, o)
    for copy in w_loads:
        copy.wait()
    whole(1, o_all).wait_recv()

    mine = o_all[slot_of(me, lax.rem(me + offset, N))].astype(jnp.float32)
    n_out = steps * seqs
    lhs = jnp.concatenate(
        [mine[h * n_out : (h + 1) * n_out, :] for h in range(heads)], 1
    ).astype(jnp.bfloat16)

    cols = w.shape[1] // PIECES
    for piece in range(PIECES):
        at = pl.ds(piece * cols, cols)
        block = jnp.dot(lhs, w[:, at], preferred_element_type=jnp.float32)
        sums[0, piece] = jnp.concatenate(
            [block[:, : cols // 2], block[:, cols // 2 :]], 0
        ).astype(jnp.bfloat16)
        for o in ORDER:
            send(2, sums, o, piece)
    whole(2, sums).wait_recv()
    for phase, slots in enumerate((q_all, o_all, sums)):
        whole(phase, slots).wait_send()


def finish(sums, res, gain, mixed_hbm, normed_hbm, mixed, normed, sems):
    steps, seqs, width = mixed_hbm.shape
    rows = steps * seqs
    parts = []
    for piece in range(PIECES):
        total = sums[0, piece].astype(jnp.float32)
        for slot in range(1, N):
            total = total + sums[slot, piece].astype(jnp.float32)
        parts += [total[:rows], total[rows:]]
    stream = jnp.concatenate(parts, 1) + res[...]
    for s in range(steps):
        mixed[s] = stream[seqs * s : seqs * (s + 1), :].astype(jnp.bfloat16)
    first = pltpu.make_async_copy(mixed, mixed_hbm, sems.at[0])
    first.start()
    spread = jnp.sum(stream * stream, -1, keepdims=True) * (1.0 / width)
    scaled = stream * lax.rsqrt(spread + 1e-05) * gain[...]
    for s in range(steps):
        normed[s] = scaled[seqs * s : seqs * (s + 1), :].astype(jnp.bfloat16)
    second = pltpu.make_async_copy(normed, normed_hbm, sems.at[1])
    second.start()
    first.wait()
    second.wait()


def pinned(array):
    if array.size == 1:
        return array
    return pltpu.with_memory_space_constraint(array, pltpu.HBM)


def shards(queries, kv_cache, fresh_kv, lengths, spare_slot, out_weight, residual, norm_gain):
    steps, seqs, width = queries.shape
    ctx = kv_cache.shape[3]
    features = out_weight.shape[1]
    heads = width // 128
    cols = features // PIECES
    bf16, f32 = jnp.bfloat16, jnp.float32
    rows = steps * seqs
    block = (2 * rows, cols // 2)
    args = [
        queries,
        kv_cache.reshape(2, seqs, ctx, 128),
        fresh_kv.reshape(2, steps, seqs, 128),
        lengths,
        spare_slot,
        out_weight,
        residual,
        norm_gain,
    ]
    sums, res, gain = pl.pallas_call(
        kernel,
        out_shape=(
            pltpu.VMEM((N, PIECES) + block, bf16),
            pltpu.VMEM((rows, features), f32),
            pltpu.VMEM((rows, features), f32),
        ),
        in_specs=[pl.BlockSpec(memory_space=pltpu.HBM)] * 8,
        out_specs=(pl.BlockSpec(memory_space=pltpu.VMEM),) * 3,
        scratch_shapes=[
            pltpu.VMEM((steps, seqs, width), bf16),
            pltpu.VMEM((ctx + PAD, seqs * 128), bf16),
            pltpu.VMEM((ctx + PAD, seqs * 128), bf16),
            pltpu.VMEM((seqs * 128, ctx + PAD), bf16),
            pltpu.VMEM((2, steps, seqs, 128), bf16),
            pltpu.SMEM((seqs,), jnp.int32),
            pltpu.SMEM((1,), jnp.int32),
            pltpu.VMEM((width, features), bf16),
            pltpu.VMEM((steps, seqs, features), bf16),
            pltpu.VMEM((features,), bf16),
            pltpu.VMEM((heads * rows, 128), f32),
            pltpu.VMEM((2, rows, 128), f32),
            pltpu.VMEM((N, heads * rows, 128), bf16),
            pltpu.VMEM((N, heads * rows, 128), bf16),
            pltpu.SemaphoreType.DMA((10,)),
            pltpu.SemaphoreType.DMA((4,)),
            pltpu.SemaphoreType.DMA((3,)),
            pltpu.SemaphoreType.DMA((3,)),
        ],
        compiler_params=pltpu.CompilerParams(
            collective_id=0, has_side_effects=True, vmem_limit_bytes=32 * 2**20
        ),
    )(*[pinned(a) for a in args])
    out = pltpu.HBM((steps, seqs, features), bf16)
    return pl.pallas_call(
        finish,
        out_shape=(out, out),
        in_specs=[pl.BlockSpec(memory_space=pltpu.VMEM)] * 3,
        out_specs=(pl.BlockSpec(memory_space=pltpu.HBM),) * 2,
        scratch_shapes=[
            pltpu.VMEM((steps, seqs, features), bf16),
            pltpu.VMEM((steps, seqs, features), bf16),
            pltpu.SemaphoreType.DMA((2,)),
        ],
        compiler_params=pltpu.CompilerParams(vmem_limit_bytes=8 * 2**20),
    )(*[pltpu.with_memory_space_constraint(a, pltpu.VMEM) for a in (sums, res, gain)])


def solution(mesh):
    return jax.shard_map(
        shards,
        mesh=mesh,
        in_specs=(
            P("replica", None, "tensor"),
            P(None, "replica", "tensor", None, None),
            P(None, None, "replica", "tensor", None),
            P("replica"),
            P("replica"),
            P("tensor", None),
            P("replica", None, None),
            P(),
        ),
        out_specs=(P("replica", None, None), P("replica", None, None)),
        check_vma=False,
    )
```

```python
import functools
import math

import jax
import jax.numpy as jnp
from jax import lax
from jax.experimental import pallas as pl
from jax.experimental.pallas import tpu as pltpu
from jax.sharding import PartitionSpec as P

N = 8
PAD = 128
WIDE = 4
PIECES = 4
ORDER = (6, 5, 7, 4, 2, 1, 3)


def partner(me, offset):
    high = lax.rem(me // 4 + offset // 4, 2)
    low = lax.rem(lax.rem(me, 4) + offset % 4, 4)
    return high * 4 + low


def slot_of(me, source):
    high = lax.rem(me // WIDE + source // WIDE, 2)
    low = lax.rem(lax.rem(me, WIDE) - lax.rem(source, WIDE) + WIDE, WIDE)
    return high * WIDE + low


def kernel(
    q_hbm, kv_hbm, fresh_hbm, len_hbm, spare_hbm, w_hbm, res_hbm, gain_hbm,
    sums, res_out, gain_out,
    q_raw, keys, values, k_turned, fresh_raw, len_s, spare_s, w, res_raw, gain_raw,
    heads_f32, fresh_f32, q_now, q_all, o_all,
    local_sem, w_sem, send_sem, recv_sem,
):
    me = lax.axis_index("tensor")
    steps, seqs, width = q_raw.shape
    heads = width // 128
    ctx = kv_hbm.shape[2]

    barrier = pltpu.get_barrier_semaphore()
    for o in ORDER:
        pl.semaphore_signal(
            barrier, inc=1, device_id={"tensor": partner(me, o)},
            device_id_type=pl.DeviceIdType.MESH,
        )

    loads = [
        pltpu.make_async_copy(q_hbm, q_raw, local_sem.at[0]),
        pltpu.make_async_copy(len_hbm, len_s, local_sem.at[1]),
        pltpu.make_async_copy(spare_hbm, spare_s, local_sem.at[2]),
        pltpu.make_async_copy(fresh_hbm, fresh_raw, local_sem.at[3]),
    ]
    for part in range(2):
        for r in range(seqs):
            loads.append(
                pltpu.make_async_copy(
                    kv_hbm.at[part, r],
                    (keys, values)[part].at[pl.ds(0, ctx), pl.ds(r * 128, 128)],
                    local_sem.at[4 + 2 * part + r],
                )
            )
    loads.append(pltpu.make_async_copy(res_hbm, res_raw, local_sem.at[8]))
    loads.append(pltpu.make_async_copy(gain_hbm, gain_raw, local_sem.at[9]))
    for copy in loads:
        copy.start()
    w_loads = []
    for piece in range(4):
        at = pl.ds(piece * w.shape[0] // 4, w.shape[0] // 4)
        copy = pltpu.make_async_copy(w_hbm.at[at], w.at[at], w_sem.at[piece])
        copy.start()
        w_loads.append(copy)

    def send(phase, slots, o, piece=None):
        src, dst = slots.at[0], slots.at[o]
        if piece is not None:
            src, dst = src.at[piece], dst.at[piece]
        copy = pltpu.make_async_remote_copy(
            src_ref=src, dst_ref=dst,
            send_sem=send_sem.at[phase], recv_sem=recv_sem.at[phase],
            device_id={"tensor": partner(me, o)},
            device_id_type=pl.DeviceIdType.MESH,
        )
        copy.start()

    def whole(phase, slots):
        others = slots.at[pl.ds(1, N - 1)]
        return pltpu.make_async_remote_copy(
            src_ref=others, dst_ref=others,
            send_sem=send_sem.at[phase], recv_sem=recv_sem.at[phase],
            device_id={"tensor": partner(me, 1)},
            device_id_type=pl.DeviceIdType.MESH,
        )

    loads[0].wait()
    n_rows = heads * steps
    for s in range(steps):
        both = q_raw[s].astype(jnp.float32)
        for h in range(heads):
            at = (h * steps + s) * seqs
            heads_f32[at : at + seqs, :] = both[:, h * 128 : (h + 1) * 128]
    q_all[0] = jnp.concatenate(
        [heads_f32[pl.ds(r, n_rows, stride=seqs), :] for r in range(seqs)], 0
    ).astype(jnp.bfloat16)
    pl.semaphore_wait(barrier, N - 1)
    for o in ORDER:
        send(0, q_all, o)

    loads[3].wait()
    for part in range(2):
        for t in range(steps):
            fresh_f32[part, 2 * t : 2 * t + 2, :] = fresh_raw[part, t].astype(jnp.float32)
    for part in range(2):
        for r in range(seqs):
            new = fresh_f32[part, pl.ds(r, steps, stride=seqs), :]
            tail = jnp.concatenate([new, jnp.zeros((PAD - steps, 128), jnp.float32)], 0)
            (keys, values)[part][ctx : ctx + PAD, r * 128 : (r + 1) * 128] = tail.astype(
                jnp.bfloat16
            )

    for r in range(seqs):
        loads[4 + r].wait()
    for low in range(0, ctx + PAD, 128):
        k_turned[:, low : low + 128] = keys[low : low + 128, :].T

    loads[8].wait()
    for s in range(steps):
        res_out[2 * s : 2 * s + 2, :] = res_raw[s].astype(jnp.float32)
    loads[9].wait()
    gain_out[...] = jnp.broadcast_to(
        gain_raw[...].astype(jnp.float32)[None, :], gain_out.shape
    )

    for r in range(seqs):
        loads[6 + r].wait()
    loads[1].wait()
    loads[2].wait()
    offset = jnp.bitwise_and(spare_s[0], N - 1)
    q_now[...] = q_all[0]

    def attention(turn, _):
        @pl.when(turn == 1)
        def _():
            whole(0, q_all).wait_recv()
            q_now[...] = q_all[slot_of(me, lax.rem(me - offset + N, N))]

        q = q_now[...]

        scale = math.log2(math.e) / math.sqrt(128)
        none = jnp.zeros((n_rows, 128), q.dtype)
        diagonal = jnp.concatenate(
            [
                jnp.concatenate([q[:n_rows], none], 1),
                jnp.concatenate([none, q[n_rows:]], 1),
            ],
            0,
        )
        row = lax.broadcasted_iota(jnp.int32, (seqs * n_rows, 1), 0)
        limit = jnp.where(row < n_rows, len_s[0], len_s[1])
        step = lax.rem(row, steps)
        top = total = out = None
        half = ctx // 2 + PAD
        for low, high in ((0, half), (half, ctx + PAD)):
            scores = jnp.dot(
                diagonal, k_turned[:, low:high], preferred_element_type=jnp.float32
            )
            end = min(high, ctx) - low
            column = lax.broadcasted_iota(jnp.int32, (seqs * n_rows, end), 1)
            masked = jnp.where(column < limit - low, scores[:, :end], -1e30)
            if high > ctx:
                column = lax.broadcasted_iota(jnp.int32, (seqs * n_rows, PAD), 1)
                recent = jnp.where(column <= step, scores[:, end:], -1e30)
                masked = jnp.concatenate([masked, recent], 1)
            highest = jnp.max(masked, -1, keepdims=True)
            if low > 0:
                highest = jnp.maximum(top, highest)
            weights = jnp.exp2((masked - highest) * scale)
            part_total = jnp.sum(weights, -1, keepdims=True)
            part_out = jnp.dot(
                weights.astype(jnp.bfloat16), values[low:high, :],
                preferred_element_type=jnp.float32,
            )
            if low > 0:
                shrink = jnp.exp2((top - highest) * scale)
                part_total = part_total + total * shrink
                part_out = part_out + out * shrink
            top, total, out = highest, part_total, part_out
        share = 1.0 / total
        for r in range(seqs):
            mine = slice(r * n_rows, (r + 1) * n_rows)
            heads_f32[pl.ds(r, n_rows, stride=seqs), :] = (
                out[mine, r * 128 : (r + 1) * 128] * share[mine]
            )
        o_all[0] = heads_f32[...].astype(jnp.bfloat16)

        return 0

    lax.fori_loop(0, 2, attention, 0)
    for o in ORDER:
        send(1, o_all, o)
    for copy in w_loads:
        copy.wait()
    def projection(turn, _):
        @pl.when(turn == 1)
        def _():
            whole(1, o_all).wait_recv()
            heads_f32[...] = o_all[slot_of(me, lax.rem(me + offset, N))].astype(jnp.float32)

        mine = heads_f32[...]
        n_out = steps * seqs
        lhs = jnp.concatenate(
            [mine[h * n_out : (h + 1) * n_out, :] for h in range(heads)], 1
        ).astype(jnp.bfloat16)

        cols = w.shape[1] // PIECES
        for piece in range(PIECES):
            at = pl.ds(piece * cols, cols)
            block = jnp.dot(lhs, w[:, at], preferred_element_type=jnp.float32)
            sums[0, piece] = jnp.concatenate(
                [block[:, : cols // 2], block[:, cols // 2 :]], 0
            ).astype(jnp.bfloat16)

            @pl.when(turn == 1)
            def _():
                for o in ORDER:
                    send(2, sums, o, piece)

        return 0

    lax.fori_loop(0, 2, projection, 0)
    whole(2, sums).wait_recv()
    for phase, slots in enumerate((q_all, o_all, sums)):
        whole(phase, slots).wait_send()


def finish(sums, res, gain, mixed_hbm, normed_hbm, mixed, normed, sems):
    steps, seqs, width = mixed_hbm.shape
    rows = steps * seqs
    parts = []
    for piece in range(PIECES):
        total = sums[0, piece].astype(jnp.float32)
        for slot in range(1, N):
            total = total + sums[slot, piece].astype(jnp.float32)
        parts += [total[:rows], total[rows:]]
    stream = jnp.concatenate(parts, 1) + res[...]
    for s in range(steps):
        mixed[s] = stream[seqs * s : seqs * (s + 1), :].astype(jnp.bfloat16)
    first = pltpu.make_async_copy(mixed, mixed_hbm, sems.at[0])
    first.start()
    spread = jnp.sum(stream * stream, -1, keepdims=True) * (1.0 / width)
    scaled = stream * lax.rsqrt(spread + 1e-05) * gain[...]
    for s in range(steps):
        normed[s] = scaled[seqs * s : seqs * (s + 1), :].astype(jnp.bfloat16)
    second = pltpu.make_async_copy(normed, normed_hbm, sems.at[1])
    second.start()
    first.wait()
    second.wait()


def pinned(array):
    if array.size == 1:
        return array
    return pltpu.with_memory_space_constraint(array, pltpu.HBM)


def shards(queries, kv_cache, fresh_kv, lengths, spare_slot, out_weight, residual, norm_gain):
    steps, seqs, width = queries.shape
    ctx = kv_cache.shape[3]
    features = out_weight.shape[1]
    heads = width // 128
    cols = features // PIECES
    bf16, f32 = jnp.bfloat16, jnp.float32
    rows = steps * seqs
    block = (2 * rows, cols // 2)
    args = [
        queries,
        kv_cache.reshape(2, seqs, ctx, 128),
        fresh_kv.reshape(2, steps, seqs, 128),
        lengths,
        spare_slot,
        out_weight,
        residual,
        norm_gain,
    ]
    sums, res, gain = pl.pallas_call(
        kernel,
        out_shape=(
            pltpu.VMEM((N, PIECES) + block, bf16),
            pltpu.VMEM((rows, features), f32),
            pltpu.VMEM((rows, features), f32),
        ),
        in_specs=[pl.BlockSpec(memory_space=pltpu.HBM)] * 8,
        out_specs=(pl.BlockSpec(memory_space=pltpu.VMEM),) * 3,
        scratch_shapes=[
            pltpu.VMEM((steps, seqs, width), bf16),
            pltpu.VMEM((ctx + PAD, seqs * 128), bf16),
            pltpu.VMEM((ctx + PAD, seqs * 128), bf16),
            pltpu.VMEM((seqs * 128, ctx + PAD), bf16),
            pltpu.VMEM((2, steps, seqs, 128), bf16),
            pltpu.SMEM((seqs,), jnp.int32),
            pltpu.SMEM((1,), jnp.int32),
            pltpu.VMEM((width, features), bf16),
            pltpu.VMEM((steps, seqs, features), bf16),
            pltpu.VMEM((features,), bf16),
            pltpu.VMEM((heads * rows, 128), f32),
            pltpu.VMEM((2, rows, 128), f32),
            pltpu.VMEM((heads * rows, 128), bf16),
            pltpu.VMEM((N, heads * rows, 128), bf16),
            pltpu.VMEM((N, heads * rows, 128), bf16),
            pltpu.SemaphoreType.DMA((10,)),
            pltpu.SemaphoreType.DMA((4,)),
            pltpu.SemaphoreType.DMA((3,)),
            pltpu.SemaphoreType.DMA((3,)),
        ],
        compiler_params=pltpu.CompilerParams(
            collective_id=0, has_side_effects=True, vmem_limit_bytes=32 * 2**20
        ),
    )(*[pinned(a) for a in args])
    out = pltpu.HBM((steps, seqs, features), bf16)
    return pl.pallas_call(
        finish,
        out_shape=(out, out),
        in_specs=[pl.BlockSpec(memory_space=pltpu.VMEM)] * 3,
        out_specs=(pl.BlockSpec(memory_space=pltpu.HBM),) * 2,
        scratch_shapes=[
            pltpu.VMEM((steps, seqs, features), bf16),
            pltpu.VMEM((steps, seqs, features), bf16),
            pltpu.SemaphoreType.DMA((2,)),
        ],
        compiler_params=pltpu.CompilerParams(vmem_limit_bytes=8 * 2**20),
    )(*[pltpu.with_memory_space_constraint(a, pltpu.VMEM) for a in (sums, res, gain)])


def solution(mesh):
    return jax.shard_map(
        shards,
        mesh=mesh,
        in_specs=(
            P("replica", None, "tensor"),
            P(None, "replica", "tensor", None, None),
            P(None, None, "replica", "tensor", None),
            P("replica"),
            P("replica"),
            P("tensor", None),
            P("replica", None, None),
            P(),
        ),
        out_specs=(P("replica", None, None), P("replica", None, None)),
        check_vma=False,
    )
```

```python
import functools
import math

import jax
import jax.numpy as jnp
from jax import lax
from jax.experimental import pallas as pl
from jax.experimental.pallas import tpu as pltpu
from jax.sharding import PartitionSpec as P

N = 8
PAD = 128
WIDE = 4
PIECES = 4
ORDER = (6, 5, 7, 4, 2, 1, 3)


def partner(me, offset):
    high = lax.rem(me // 4 + offset // 4, 2)
    low = lax.rem(lax.rem(me, 4) + offset % 4, 4)
    return high * 4 + low


def slot_of(me, source):
    high = lax.rem(me // WIDE + source // WIDE, 2)
    low = lax.rem(lax.rem(me, WIDE) - lax.rem(source, WIDE) + WIDE, WIDE)
    return high * WIDE + low


def kernel(
    q_hbm, kv_hbm, fresh_hbm, len_hbm, spare_hbm, w_hbm, res_hbm, gain_hbm,
    sums, res_out, gain_out,
    q_raw, keys, values, k_turned, fresh_raw, len_s, spare_s, w, res_raw, gain_raw,
    heads_f32, fresh_f32, q_now, q_all, o_all,
    local_sem, w_sem, send_sem, recv_sem,
):
    me = lax.axis_index("tensor")
    steps, seqs, width = q_raw.shape
    heads = width // 128
    ctx = kv_hbm.shape[2]

    barrier = pltpu.get_barrier_semaphore()
    for o in ORDER:
        pl.semaphore_signal(
            barrier, inc=1, device_id={"tensor": partner(me, o)},
            device_id_type=pl.DeviceIdType.MESH,
        )

    loads = [
        pltpu.make_async_copy(q_hbm, q_raw, local_sem.at[0]),
        pltpu.make_async_copy(len_hbm, len_s, local_sem.at[1]),
        pltpu.make_async_copy(spare_hbm, spare_s, local_sem.at[2]),
        pltpu.make_async_copy(fresh_hbm, fresh_raw, local_sem.at[3]),
    ]
    for part in range(2):
        for r in range(seqs):
            loads.append(
                pltpu.make_async_copy(
                    kv_hbm.at[part, r],
                    (keys, values)[part].at[pl.ds(0, ctx), pl.ds(r * 128, 128)],
                    local_sem.at[4 + 2 * part + r],
                )
            )
    loads.append(pltpu.make_async_copy(res_hbm, res_raw, local_sem.at[8]))
    loads.append(pltpu.make_async_copy(gain_hbm, gain_raw, local_sem.at[9]))
    for copy in loads:
        copy.start()
    w_loads = []
    for piece in range(4):
        at = pl.ds(piece * w.shape[0] // 4, w.shape[0] // 4)
        copy = pltpu.make_async_copy(w_hbm.at[at], w.at[at], w_sem.at[piece])
        copy.start()
        w_loads.append(copy)

    def send(phase, slots, o, piece=None):
        src, dst = slots.at[0], slots.at[o]
        if piece is not None:
            src, dst = src.at[piece], dst.at[piece]
        copy = pltpu.make_async_remote_copy(
            src_ref=src, dst_ref=dst,
            send_sem=send_sem.at[phase], recv_sem=recv_sem.at[phase],
            device_id={"tensor": partner(me, o)},
            device_id_type=pl.DeviceIdType.MESH,
        )
        copy.start()

    def whole(phase, slots):
        others = slots.at[pl.ds(1, N - 1)]
        return pltpu.make_async_remote_copy(
            src_ref=others, dst_ref=others,
            send_sem=send_sem.at[phase], recv_sem=recv_sem.at[phase],
            device_id={"tensor": partner(me, 1)},
            device_id_type=pl.DeviceIdType.MESH,
        )

    loads[0].wait()
    n_rows = heads * steps
    for s in range(steps):
        both = q_raw[s].astype(jnp.float32)
        for h in range(heads):
            at = (h * steps + s) * seqs
            heads_f32[at : at + seqs, :] = both[:, h * 128 : (h + 1) * 128]
    q_all[0] = jnp.concatenate(
        [heads_f32[pl.ds(r, n_rows, stride=seqs), :] for r in range(seqs)], 0
    ).astype(jnp.bfloat16)
    pl.semaphore_wait(barrier, N - 1)
    for o in ORDER:
        send(0, q_all, o)

    loads[3].wait()
    for part in range(2):
        for t in range(steps):
            fresh_f32[part, 2 * t : 2 * t + 2, :] = fresh_raw[part, t].astype(jnp.float32)
    for part in range(2):
        for r in range(seqs):
            new = fresh_f32[part, pl.ds(r, steps, stride=seqs), :]
            tail = jnp.concatenate([new, jnp.zeros((PAD - steps, 128), jnp.float32)], 0)
            (keys, values)[part][ctx : ctx + PAD, r * 128 : (r + 1) * 128] = tail.astype(
                jnp.bfloat16
            )

    for r in range(seqs):
        loads[4 + r].wait()
    for low in range(0, ctx + PAD, 128):
        k_turned[:, low : low + 128] = keys[low : low + 128, :].T

    loads[8].wait()
    for s in range(steps):
        res_out[2 * s : 2 * s + 2, :] = res_raw[s].astype(jnp.float32)
    loads[9].wait()
    gain_out[...] = jnp.broadcast_to(
        gain_raw[...].astype(jnp.float32)[None, :], gain_out.shape
    )

    for r in range(seqs):
        loads[6 + r].wait()
    loads[1].wait()
    loads[2].wait()
    offset = jnp.bitwise_and(spare_s[0], N - 1)
    q_now[...] = q_all[0]

    def attention(turn, _):
        @pl.when(turn == 1)
        def _():
            whole(0, q_all).wait_recv()
            q_now[...] = q_all[slot_of(me, lax.rem(me - offset + N, N))]

        q = q_now[...]

        scale = math.log2(math.e) / math.sqrt(128)
        none = jnp.zeros((n_rows, 128), q.dtype)
        diagonal = jnp.concatenate(
            [
                jnp.concatenate([q[:n_rows], none], 1),
                jnp.concatenate([none, q[n_rows:]], 1),
            ],
            0,
        )
        row = lax.broadcasted_iota(jnp.int32, (seqs * n_rows, 1), 0)
        limit = jnp.where(row < n_rows, len_s[0], len_s[1])
        step = lax.rem(row, steps)
        top = total = out = None
        half = ctx // 2 + PAD
        for low, high in ((0, half), (half, ctx + PAD)):
            scores = jnp.dot(
                diagonal, k_turned[:, low:high], preferred_element_type=jnp.float32
            )
            end = min(high, ctx) - low
            column = lax.broadcasted_iota(jnp.int32, (seqs * n_rows, end), 1)
            masked = jnp.where(column < limit - low, scores[:, :end], -1e30)
            if high > ctx:
                column = lax.broadcasted_iota(jnp.int32, (seqs * n_rows, PAD), 1)
                recent = jnp.where(column <= step, scores[:, end:], -1e30)
                masked = jnp.concatenate([masked, recent], 1)
            highest = jnp.max(masked, -1, keepdims=True)
            if low > 0:
                highest = jnp.maximum(top, highest)
            weights = jnp.exp2((masked - highest) * scale)
            part_total = jnp.sum(weights, -1, keepdims=True)
            part_out = jnp.dot(
                weights.astype(jnp.bfloat16), values[low:high, :],
                preferred_element_type=jnp.float32,
            )
            if low > 0:
                shrink = jnp.exp2((top - highest) * scale)
                part_total = part_total + total * shrink
                part_out = part_out + out * shrink
            top, total, out = highest, part_total, part_out
        share = 1.0 / total
        for r in range(seqs):
            mine = slice(r * n_rows, (r + 1) * n_rows)
            heads_f32[pl.ds(r, n_rows, stride=seqs), :] = (
                out[mine, r * 128 : (r + 1) * 128] * share[mine]
            )
        o_all[0] = heads_f32[...].astype(jnp.bfloat16)

        return 0

    lax.fori_loop(0, 2, attention, 0)
    for o in ORDER:
        send(1, o_all, o)
    for copy in w_loads:
        copy.wait()
    cols = w.shape[1] // PIECES
    n_out = steps * seqs

    def project(turn, _):
        @pl.when(turn == 1)
        def _():
            whole(1, o_all).wait_recv()
            heads_f32[...] = o_all[slot_of(me, lax.rem(me + offset, N))].astype(jnp.float32)

        mine = heads_f32[...]
        lhs = jnp.concatenate(
            [mine[h * n_out : (h + 1) * n_out, :] for h in range(heads)], 1
        ).astype(jnp.bfloat16)
        piece = lax.rem(turn + PIECES - 1, PIECES)
        at = pl.ds(pl.multiple_of(piece * cols, cols), cols)
        block = jnp.dot(lhs, w[:, at], preferred_element_type=jnp.float32)
        sums[0, piece] = jnp.concatenate(
            [block[:, : cols // 2], block[:, cols // 2 :]], 0
        ).astype(jnp.bfloat16)

        @pl.when(turn > 0)
        def _():
            for o in ORDER:
                send(2, sums, o, piece)

        return 0

    lax.fori_loop(0, PIECES + 1, project, 0)
    whole(2, sums).wait_recv()
    for phase, slots in enumerate((q_all, o_all, sums)):
        whole(phase, slots).wait_send()


def finish(sums, res, gain, mixed_hbm, normed_hbm, mixed, normed, sems):
    steps, seqs, width = mixed_hbm.shape
    rows = steps * seqs
    parts = []
    for piece in range(PIECES):
        total = sums[0, piece].astype(jnp.float32)
        for slot in range(1, N):
            total = total + sums[slot, piece].astype(jnp.float32)
        parts += [total[:rows], total[rows:]]
    stream = jnp.concatenate(parts, 1) + res[...]
    for s in range(steps):
        mixed[s] = stream[seqs * s : seqs * (s + 1), :].astype(jnp.bfloat16)
    first = pltpu.make_async_copy(mixed, mixed_hbm, sems.at[0])
    first.start()
    spread = jnp.sum(stream * stream, -1, keepdims=True) * (1.0 / width)
    scaled = stream * lax.rsqrt(spread + 1e-05) * gain[...]
    for s in range(steps):
        normed[s] = scaled[seqs * s : seqs * (s + 1), :].astype(jnp.bfloat16)
    second = pltpu.make_async_copy(normed, normed_hbm, sems.at[1])
    second.start()
    first.wait()
    second.wait()


def pinned(array):
    if array.size == 1:
        return array
    return pltpu.with_memory_space_constraint(array, pltpu.HBM)


def shards(queries, kv_cache, fresh_kv, lengths, spare_slot, out_weight, residual, norm_gain):
    steps, seqs, width = queries.shape
    ctx = kv_cache.shape[3]
    features = out_weight.shape[1]
    heads = width // 128
    cols = features // PIECES
    bf16, f32 = jnp.bfloat16, jnp.float32
    rows = steps * seqs
    block = (2 * rows, cols // 2)
    args = [
        queries,
        kv_cache.reshape(2, seqs, ctx, 128),
        fresh_kv.reshape(2, steps, seqs, 128),
        lengths,
        spare_slot,
        out_weight,
        residual,
        norm_gain,
    ]
    sums, res, gain = pl.pallas_call(
        kernel,
        out_shape=(
            pltpu.VMEM((N, PIECES) + block, bf16),
            pltpu.VMEM((rows, features), f32),
            pltpu.VMEM((rows, features), f32),
        ),
        in_specs=[pl.BlockSpec(memory_space=pltpu.HBM)] * 8,
        out_specs=(pl.BlockSpec(memory_space=pltpu.VMEM),) * 3,
        scratch_shapes=[
            pltpu.VMEM((steps, seqs, width), bf16),
            pltpu.VMEM((ctx + PAD, seqs * 128), bf16),
            pltpu.VMEM((ctx + PAD, seqs * 128), bf16),
            pltpu.VMEM((seqs * 128, ctx + PAD), bf16),
            pltpu.VMEM((2, steps, seqs, 128), bf16),
            pltpu.SMEM((seqs,), jnp.int32),
            pltpu.SMEM((1,), jnp.int32),
            pltpu.VMEM((width, features), bf16),
            pltpu.VMEM((steps, seqs, features), bf16),
            pltpu.VMEM((features,), bf16),
            pltpu.VMEM((heads * rows, 128), f32),
            pltpu.VMEM((2, rows, 128), f32),
            pltpu.VMEM((heads * rows, 128), bf16),
            pltpu.VMEM((N, heads * rows, 128), bf16),
            pltpu.VMEM((N, heads * rows, 128), bf16),
            pltpu.SemaphoreType.DMA((10,)),
            pltpu.SemaphoreType.DMA((4,)),
            pltpu.SemaphoreType.DMA((3,)),
            pltpu.SemaphoreType.DMA((3,)),
        ],
        compiler_params=pltpu.CompilerParams(
            collective_id=0, has_side_effects=True, vmem_limit_bytes=32 * 2**20
        ),
    )(*[pinned(a) for a in args])
    out = pltpu.HBM((steps, seqs, features), bf16)
    return pl.pallas_call(
        finish,
        out_shape=(out, out),
        in_specs=[pl.BlockSpec(memory_space=pltpu.VMEM)] * 3,
        out_specs=(pl.BlockSpec(memory_space=pltpu.HBM),) * 2,
        scratch_shapes=[
            pltpu.VMEM((steps, seqs, features), bf16),
            pltpu.VMEM((steps, seqs, features), bf16),
            pltpu.SemaphoreType.DMA((2,)),
        ],
        compiler_params=pltpu.CompilerParams(vmem_limit_bytes=8 * 2**20),
    )(*[pltpu.with_memory_space_constraint(a, pltpu.VMEM) for a in (sums, res, gain)])


def solution(mesh):
    return jax.shard_map(
        shards,
        mesh=mesh,
        in_specs=(
            P("replica", None, "tensor"),
            P(None, "replica", "tensor", None, None),
            P(None, None, "replica", "tensor", None),
            P("replica"),
            P("replica"),
            P("tensor", None),
            P("replica", None, None),
            P(),
        ),
        out_specs=(P("replica", None, None), P("replica", None, None)),
        check_vma=False,
    )
```

```python
import functools
import math

import jax
import jax.numpy as jnp
from jax import lax
from jax.experimental import pallas as pl
from jax.experimental.pallas import tpu as pltpu
from jax.sharding import PartitionSpec as P

N = 8
PAD = 128
WIDE = 4
PIECES = 4
ACROSS, ALONG_X = (6, 5, 7, 4), (2, 1, 3)
ORDER = ACROSS + ALONG_X


def partner(me, offset):
    high = lax.rem(me // 4 + offset // 4, 2)
    low = lax.rem(lax.rem(me, 4) + offset % 4, 4)
    return high * 4 + low


def slot_of(me, source):
    high = lax.rem(me // WIDE + source // WIDE, 2)
    low = lax.rem(lax.rem(me, WIDE) - lax.rem(source, WIDE) + WIDE, WIDE)
    return high * WIDE + low


def kernel(
    q_hbm, kv_hbm, fresh_hbm, len_hbm, spare_hbm, w_hbm, res_hbm, gain_hbm,
    sums, res_out, gain_out,
    q_raw, keys, values, k_turned, fresh_raw, len_s, spare_s, w, res_raw, gain_raw,
    heads_f32, fresh_f32, q_now, q_all, o_all,
    local_sem, w_sem, send_sem, recv_sem,
):
    me = lax.axis_index("tensor")
    steps, seqs, width = q_raw.shape
    heads = width // 128
    ctx = kv_hbm.shape[2]

    barrier = pltpu.get_barrier_semaphore()
    for o in ORDER:
        pl.semaphore_signal(
            barrier, inc=1, device_id={"tensor": partner(me, o)},
            device_id_type=pl.DeviceIdType.MESH,
        )

    loads = [
        pltpu.make_async_copy(q_hbm, q_raw, local_sem.at[0]),
        pltpu.make_async_copy(len_hbm, len_s, local_sem.at[1]),
        pltpu.make_async_copy(spare_hbm, spare_s, local_sem.at[2]),
        pltpu.make_async_copy(fresh_hbm, fresh_raw, local_sem.at[3]),
    ]
    for part in range(2):
        for r in range(seqs):
            loads.append(
                pltpu.make_async_copy(
                    kv_hbm.at[part, r],
                    (keys, values)[part].at[pl.ds(0, ctx), pl.ds(r * 128, 128)],
                    local_sem.at[4 + 2 * part + r],
                )
            )
    loads.append(pltpu.make_async_copy(res_hbm, res_raw, local_sem.at[8]))
    loads.append(pltpu.make_async_copy(gain_hbm, gain_raw, local_sem.at[9]))
    for copy in loads:
        copy.start()
    w_loads = []
    for piece in range(4):
        at = pl.ds(piece * w.shape[0] // 4, w.shape[0] // 4)
        copy = pltpu.make_async_copy(w_hbm.at[at], w.at[at], w_sem.at[piece])
        copy.start()
        w_loads.append(copy)

    def send(phase, slots, o, piece=None):
        src, dst = slots.at[0], slots.at[o]
        if piece is not None:
            src, dst = src.at[piece], dst.at[piece]
        copy = pltpu.make_async_remote_copy(
            src_ref=src, dst_ref=dst,
            send_sem=send_sem.at[phase], recv_sem=recv_sem.at[phase],
            device_id={"tensor": partner(me, o)},
            device_id_type=pl.DeviceIdType.MESH,
        )
        copy.start()

    def whole(phase, slots):
        others = slots.at[pl.ds(1, N - 1)]
        return pltpu.make_async_remote_copy(
            src_ref=others, dst_ref=others,
            send_sem=send_sem.at[phase], recv_sem=recv_sem.at[phase],
            device_id={"tensor": partner(me, 1)},
            device_id_type=pl.DeviceIdType.MESH,
        )

    loads[0].wait()
    n_rows = heads * steps
    for s in range(steps):
        both = q_raw[s].astype(jnp.float32)
        for h in range(heads):
            at = (h * steps + s) * seqs
            heads_f32[at : at + seqs, :] = both[:, h * 128 : (h + 1) * 128]
    q_all[0] = jnp.concatenate(
        [heads_f32[pl.ds(r, n_rows, stride=seqs), :] for r in range(seqs)], 0
    ).astype(jnp.bfloat16)
    pl.semaphore_wait(barrier, N - 1)
    for o in ORDER:
        send(0, q_all, o)

    loads[3].wait()
    for part in range(2):
        for t in range(steps):
            fresh_f32[part, 2 * t : 2 * t + 2, :] = fresh_raw[part, t].astype(jnp.float32)
    for part in range(2):
        for r in range(seqs):
            new = fresh_f32[part, pl.ds(r, steps, stride=seqs), :]
            tail = jnp.concatenate([new, jnp.zeros((PAD - steps, 128), jnp.float32)], 0)
            (keys, values)[part][ctx : ctx + PAD, r * 128 : (r + 1) * 128] = tail.astype(
                jnp.bfloat16
            )

    for r in range(seqs):
        loads[4 + r].wait()
    for low in range(0, ctx + PAD, 128):
        k_turned[:, low : low + 128] = keys[low : low + 128, :].T

    loads[8].wait()
    for s in range(steps):
        res_out[2 * s : 2 * s + 2, :] = res_raw[s].astype(jnp.float32)
    loads[9].wait()
    gain_out[...] = jnp.broadcast_to(
        gain_raw[...].astype(jnp.float32)[None, :], gain_out.shape
    )

    for r in range(seqs):
        loads[6 + r].wait()
    loads[1].wait()
    loads[2].wait()
    offset = jnp.bitwise_and(spare_s[0], N - 1)
    q_now[...] = q_all[0]

    def attention(turn, _):
        @pl.when(turn == 1)
        def _():
            whole(0, q_all).wait_recv()
            q_now[...] = q_all[slot_of(me, lax.rem(me - offset + N, N))]

        q = q_now[...]

        scale = math.log2(math.e) / math.sqrt(128)
        none = jnp.zeros((n_rows, 128), q.dtype)
        diagonal = jnp.concatenate(
            [
                jnp.concatenate([q[:n_rows], none], 1),
                jnp.concatenate([none, q[n_rows:]], 1),
            ],
            0,
        )
        row = lax.broadcasted_iota(jnp.int32, (seqs * n_rows, 1), 0)
        limit = jnp.where(row < n_rows, len_s[0], len_s[1])
        step = lax.rem(row, steps)
        top = total = out = None
        half = ctx // 2 + PAD
        for low, high in ((0, half), (half, ctx + PAD)):
            scores = jnp.dot(
                diagonal, k_turned[:, low:high], preferred_element_type=jnp.float32
            )
            end = min(high, ctx) - low
            column = lax.broadcasted_iota(jnp.int32, (seqs * n_rows, end), 1)
            masked = jnp.where(column < limit - low, scores[:, :end], -1e30)
            if high > ctx:
                column = lax.broadcasted_iota(jnp.int32, (seqs * n_rows, PAD), 1)
                recent = jnp.where(column <= step, scores[:, end:], -1e30)
                masked = jnp.concatenate([masked, recent], 1)
            highest = jnp.max(masked, -1, keepdims=True)
            if low > 0:
                highest = jnp.maximum(top, highest)
            weights = jnp.exp2((masked - highest) * scale)
            part_total = jnp.sum(weights, -1, keepdims=True)
            part_out = jnp.dot(
                weights.astype(jnp.bfloat16), values[low:high, :],
                preferred_element_type=jnp.float32,
            )
            if low > 0:
                shrink = jnp.exp2((top - highest) * scale)
                part_total = part_total + total * shrink
                part_out = part_out + out * shrink
            top, total, out = highest, part_total, part_out
        share = 1.0 / total
        for r in range(seqs):
            mine = slice(r * n_rows, (r + 1) * n_rows)
            heads_f32[pl.ds(r, n_rows, stride=seqs), :] = (
                out[mine, r * 128 : (r + 1) * 128] * share[mine]
            )
        o_all[0] = heads_f32[...].astype(jnp.bfloat16)

        return 0

    lax.fori_loop(0, 2, attention, 0)
    for o in ORDER:
        send(1, o_all, o)
    for copy in w_loads:
        copy.wait()
    cols = w.shape[1] // PIECES
    n_out = steps * seqs

    def project(turn, _):
        @pl.when(turn == 1)
        def _():
            whole(1, o_all).wait_recv()
            heads_f32[...] = o_all[slot_of(me, lax.rem(me + offset, N))].astype(jnp.float32)

        mine = heads_f32[...]
        lhs = jnp.concatenate(
            [mine[h * n_out : (h + 1) * n_out, :] for h in range(heads)], 1
        ).astype(jnp.bfloat16)
        piece = lax.rem(turn + PIECES - 1, PIECES)
        at = pl.ds(pl.multiple_of(piece * cols, cols), cols)
        block = jnp.dot(lhs, w[:, at], preferred_element_type=jnp.float32)
        sums[0, piece] = jnp.concatenate(
            [block[:, : cols // 2], block[:, cols // 2 :]], 0
        ).astype(jnp.bfloat16)

        @pl.when(turn > 0)
        def _():
            for o in ACROSS:
                send(2, sums, o, piece)

        return 0

    lax.fori_loop(0, PIECES + 1, project, 0)
    for o in ALONG_X:
        send(2, sums, o)
    whole(2, sums).wait_recv()
    for phase, slots in enumerate((q_all, o_all, sums)):
        whole(phase, slots).wait_send()


def finish(sums, res, gain, mixed_hbm, normed_hbm, mixed, normed, sems):
    steps, seqs, width = mixed_hbm.shape
    rows = steps * seqs
    parts = []
    for piece in range(PIECES):
        total = sums[0, piece].astype(jnp.float32)
        for slot in range(1, N):
            total = total + sums[slot, piece].astype(jnp.float32)
        parts += [total[:rows], total[rows:]]
    stream = jnp.concatenate(parts, 1) + res[...]
    for s in range(steps):
        mixed[s] = stream[seqs * s : seqs * (s + 1), :].astype(jnp.bfloat16)
    first = pltpu.make_async_copy(mixed, mixed_hbm, sems.at[0])
    first.start()
    spread = jnp.sum(stream * stream, -1, keepdims=True) * (1.0 / width)
    scaled = stream * lax.rsqrt(spread + 1e-05) * gain[...]
    for s in range(steps):
        normed[s] = scaled[seqs * s : seqs * (s + 1), :].astype(jnp.bfloat16)
    second = pltpu.make_async_copy(normed, normed_hbm, sems.at[1])
    second.start()
    first.wait()
    second.wait()


def pinned(array):
    if array.size == 1:
        return array
    return pltpu.with_memory_space_constraint(array, pltpu.HBM)


def shards(queries, kv_cache, fresh_kv, lengths, spare_slot, out_weight, residual, norm_gain):
    steps, seqs, width = queries.shape
    ctx = kv_cache.shape[3]
    features = out_weight.shape[1]
    heads = width // 128
    cols = features // PIECES
    bf16, f32 = jnp.bfloat16, jnp.float32
    rows = steps * seqs
    block = (2 * rows, cols // 2)
    args = [
        queries,
        kv_cache.reshape(2, seqs, ctx, 128),
        fresh_kv.reshape(2, steps, seqs, 128),
        lengths,
        spare_slot,
        out_weight,
        residual,
        norm_gain,
    ]
    sums, res, gain = pl.pallas_call(
        kernel,
        out_shape=(
            pltpu.VMEM((N, PIECES) + block, bf16),
            pltpu.VMEM((rows, features), f32),
            pltpu.VMEM((rows, features), f32),
        ),
        in_specs=[pl.BlockSpec(memory_space=pltpu.HBM)] * 8,
        out_specs=(pl.BlockSpec(memory_space=pltpu.VMEM),) * 3,
        scratch_shapes=[
            pltpu.VMEM((steps, seqs, width), bf16),
            pltpu.VMEM((ctx + PAD, seqs * 128), bf16),
            pltpu.VMEM((ctx + PAD, seqs * 128), bf16),
            pltpu.VMEM((seqs * 128, ctx + PAD), bf16),
            pltpu.VMEM((2, steps, seqs, 128), bf16),
            pltpu.SMEM((seqs,), jnp.int32),
            pltpu.SMEM((1,), jnp.int32),
            pltpu.VMEM((width, features), bf16),
            pltpu.VMEM((steps, seqs, features), bf16),
            pltpu.VMEM((features,), bf16),
            pltpu.VMEM((heads * rows, 128), f32),
            pltpu.VMEM((2, rows, 128), f32),
            pltpu.VMEM((heads * rows, 128), bf16),
            pltpu.VMEM((N, heads * rows, 128), bf16),
            pltpu.VMEM((N, heads * rows, 128), bf16),
            pltpu.SemaphoreType.DMA((10,)),
            pltpu.SemaphoreType.DMA((4,)),
            pltpu.SemaphoreType.DMA((3,)),
            pltpu.SemaphoreType.DMA((3,)),
        ],
        compiler_params=pltpu.CompilerParams(
            collective_id=0, has_side_effects=True, vmem_limit_bytes=32 * 2**20
        ),
    )(*[pinned(a) for a in args])
    out = pltpu.HBM((steps, seqs, features), bf16)
    return pl.pallas_call(
        finish,
        out_shape=(out, out),
        in_specs=[pl.BlockSpec(memory_space=pltpu.VMEM)] * 3,
        out_specs=(pl.BlockSpec(memory_space=pltpu.HBM),) * 2,
        scratch_shapes=[
            pltpu.VMEM((steps, seqs, features), bf16),
            pltpu.VMEM((steps, seqs, features), bf16),
            pltpu.SemaphoreType.DMA((2,)),
        ],
        compiler_params=pltpu.CompilerParams(vmem_limit_bytes=8 * 2**20),
    )(*[pltpu.with_memory_space_constraint(a, pltpu.VMEM) for a in (sums, res, gain)])


def solution(mesh):
    return jax.shard_map(
        shards,
        mesh=mesh,
        in_specs=(
            P("replica", None, "tensor"),
            P(None, "replica", "tensor", None, None),
            P(None, None, "replica", "tensor", None),
            P("replica"),
            P("replica"),
            P("tensor", None),
            P("replica", None, None),
            P(),
        ),
        out_specs=(P("replica", None, None), P("replica", None, None)),
        check_vma=False,
    )
```
